512 devices in a mesh: gx: 32 (over x_lo, z), gy: 16 (over y, x_hi, core).
Axes of the slice: x: 4 (x_hi: 2, x_lo: 2; x = x_hi * 2 + x_lo), y: 4, z: 16, core: 2. Of those that a mesh axis runs over, the one named last changes fastest.
Arguments:
- e_field: float32 [6, 20, 256, 2048], P(None, None, 'gx', 'gy'), may hold values from -6 to 6
- h_field: float32 [6, 20, 256, 2048], P(None, None, 'gx', 'gy'), may hold values from -6 to 6
- material: int32 [20, 256, 2048], P(None, 'gx', 'gy'), may hold values from 0 to 7
- eps_table: float32 [8], replicated, may hold values from 1 to 12
- bloch_phase: float32 [2], replicated, may hold values from 0.3 to 2.8
- orders: int32 [2, 4096], replicated, may hold values from -32 to 31
Outputs:
- e_next: float32 [6, 20, 256, 2048], P(None, None, 'gx', 'gy')
- h_next: float32 [6, 20, 256, 2048], P(None, None, 'gx', 'gy')
- amplitudes: float32 [4, 4096], P(None, ('gx', 'gy'))
The draws below stay inside these ranges and needn't reach their ends.
Inputs may be any that keep to these rules, and one draw needn't show every extreme that they name: material indices name entries of eps_table. `orders`: order indices may repeat.
All inputs are finite; a program needn't handle non-finite values.
Results may differ from the reference program's by a relative error of at most 0.0001.
Values sent between devices are 32-bit elements; how exact they have to be, the bound alone decides.
A program may use at most 128 MiB of HBM per device.

```python
import math
import jax
import jax.numpy as jnp
from jax import lax

Z = 20
STEPS = 4
NMAT = 8
NORD = 4096
NX = 256
NY = 2048


def touch_ends(drawn, stream_key, least, top_value):
    dims = drawn.shape
    spot = [jax.random.randint(jax.random.fold_in(stream_key, axis), (), 0, dims[axis]) for axis in range(len(dims))]
    drawn = drawn.at[tuple(spot)].set(least)
    longest = dims.index(max(dims))
    spot[longest] = (spot[longest] + 1) % dims[longest]
    return drawn.at[tuple(spot)].set(top_value)


def block_scale(key, extent, cuts, least, high):
    gain = 1.0
    for position, shards_of in cuts:
        draws = jax.random.uniform(jax.random.fold_in(jax.random.fold_in(key, 6), position), (shards_of,), jnp.float32, least / len(cuts), high / len(cuts))
        gain = gain * jnp.repeat(jnp.exp(draws), extent[position] // shards_of).reshape((-1,) + (1,) * (len(extent) - 1 - position))
    return gain


def normal_values(stream_key, dims, scale, limit, cuts=(), kind=jnp.bfloat16):
    level = block_scale(stream_key, dims, cuts, -0.22, 0.18) if cuts else 1.0
    result = jax.random.normal(stream_key, dims, jnp.float32) * scale * level
    return jnp.minimum(jnp.maximum(result, -limit), limit).astype(kind)


def setup_inputs(seed: int = 0) -> dict:
    streams_of = jax.random.split(jax.random.key(seed), 7)
    e_field = normal_values(streams_of[0], (6, Z, NX, NY), 1.0, 6.0, ((2, 32), (3, 16)), jnp.float32)
    h_field = normal_values(streams_of[1], (6, Z, NX, NY), 1.0, 6.0, ((2, 32), (3, 16)), jnp.float32)
    material = touch_ends(jax.random.randint(streams_of[2], (Z, NX, NY), 0, NMAT), jax.random.fold_in(streams_of[2], 1), 0, NMAT - 1).astype(jnp.int32)
    eps_table = jnp.clip(jnp.exp(jax.random.uniform(streams_of[3], (NMAT,), jnp.float32, math.log(1.0), math.log(12.0))), 1.0, 12.0)
    bloch_phase = jnp.clip(jax.random.uniform(streams_of[4], (2,), jnp.float32, 0.3, 2.8), 0.3, 2.8)
    orders = touch_ends(jax.random.randint(streams_of[5], (2, NORD), -32, 32), jax.random.fold_in(streams_of[5], 1), -32, 31).astype(jnp.int32)
    return {"e_field": e_field, "h_field": h_field, "material": material, "eps_table": eps_table, "bloch_phase": bloch_phase, "orders": orders}


DT_STEP = 0.5

def wrap_ahead(field, axis, phase):
    cosine = jnp.cos(phase)
    sine = jnp.sin(phase)
    first = lax.slice_in_dim(field, 0, 1, axis=axis)
    rest = lax.slice_in_dim(field, 1, field.shape[axis], axis=axis)
    wrapped = jnp.concatenate([cosine * first[:3] - sine * first[3:], sine * first[:3] + cosine * first[3:]], 0)
    return jnp.concatenate([rest, wrapped], axis)

def wrap_behind(field, axis, phase):
    cosine = jnp.cos(phase)
    sine = jnp.sin(phase)
    count = field.shape[axis]
    last = lax.slice_in_dim(field, count - 1, count, axis=axis)
    rest = lax.slice_in_dim(field, 0, count - 1, axis=axis)
    wrapped = jnp.concatenate([cosine * last[:3] + sine * last[3:], cosine * last[3:] - sine * last[:3]], 0)
    return jnp.concatenate([wrapped, rest], axis)

def z_ahead(field):
    return jnp.concatenate([field[:, 1:], jnp.zeros_like(field[:, :1])], 1)

def z_behind(field):
    return jnp.concatenate([jnp.zeros_like(field[:, :1]), field[:, :-1]], 1)

def curl_of_e(field, ahead_x, ahead_y, ahead_z):
    parts = []
    for offset in (0, 3):
        parts.append(ahead_y[offset + 2] - field[offset + 2] - (ahead_z[offset + 1] - field[offset + 1]))
        parts.append(ahead_z[offset] - field[offset] - (ahead_x[offset + 2] - field[offset + 2]))
        parts.append(ahead_x[offset + 1] - field[offset + 1] - (ahead_y[offset] - field[offset]))
    return jnp.stack(parts)

def curl_of_h(field, behind_x, behind_y, behind_z):
    parts = []
    for offset in (0, 3):
        parts.append(field[offset + 2] - behind_y[offset + 2] - (field[offset + 1] - behind_z[offset + 1]))
        parts.append(field[offset] - behind_z[offset] - (field[offset + 2] - behind_x[offset + 2]))
        parts.append(field[offset + 1] - behind_x[offset + 1] - (field[offset] - behind_y[offset]))
    return jnp.stack(parts)

def project(reals, imags, orders, phase_x, phase_y, start_x, start_y, total_x, total_y):
    highest = lax.Precision.HIGHEST
    along_x = start_x + jnp.arange(reals.shape[1], dtype=jnp.int32)
    along_y = start_y + jnp.arange(reals.shape[2], dtype=jnp.int32)
    wrap_x = orders[0][:, None] * along_x[None, :] % total_x
    wrap_y = orders[1][:, None] * along_y[None, :] % total_y
    angle_x = 2.0 * math.pi * wrap_x.astype(jnp.float32) / total_x + phase_x * along_x.astype(jnp.float32)[None, :] / total_x
    angle_y = 2.0 * math.pi * wrap_y.astype(jnp.float32) / total_y + phase_y * along_y.astype(jnp.float32)[None, :] / total_y
    cos_x = jnp.cos(angle_x)
    sin_x = jnp.sin(angle_x)
    cos_y = jnp.cos(angle_y)
    sin_y = jnp.sin(angle_y)
    rows = []
    for comp in (0, 1):
        part_re = jnp.dot(cos_x, reals[comp], precision=highest) + jnp.dot(sin_x, imags[comp], precision=highest)
        part_im = jnp.dot(cos_x, imags[comp], precision=highest) - jnp.dot(sin_x, reals[comp], precision=highest)
        rows.append(lax.optimization_barrier(jnp.sum(part_re * cos_y + part_im * sin_y, 1)))
        rows.append(lax.optimization_barrier(jnp.sum(part_im * cos_y - part_re * sin_y, 1)))
    return jnp.stack(rows) / math.sqrt(total_x * total_y)

def reference(e_field, h_field, material, eps_table, bloch_phase, orders):
    coef = DT_STEP / eps_table[material]
    phase_x = bloch_phase[0]
    phase_y = bloch_phase[1]
    for number in range(STEPS):
        h_field = h_field - DT_STEP * curl_of_e(e_field, wrap_ahead(e_field, 2, phase_x), wrap_ahead(e_field, 3, phase_y), z_ahead(e_field))
        e_field = e_field + coef[None] * curl_of_h(h_field, wrap_behind(h_field, 2, phase_x), wrap_behind(h_field, 3, phase_y), z_behind(h_field))
    plane = e_field[:, e_field.shape[1] - 2]
    amplitudes = project(plane[0:2], plane[3:5], orders, phase_x, phase_y, 0, 0, NX, NY)
    return (e_field, h_field, amplitudes)
```

```python
import math

import jax
import jax.numpy as jnp
from jax import lax
from jax.experimental import pallas as pl
from jax.experimental.pallas import tpu as pltpu
from jax.sharding import PartitionSpec as P

MESH = pl.DeviceIdType.MESH
F32 = jnp.float32

STEPS = 4
Z = 20
NX = 256
NY = 2048
GX = 32
GY = 16
RING = 16
HALVES = GX // RING
PLANE = HALVES * GY
CX = NX // GX
CY = NY // GY
SPAN = 64
TOP = 14
COEF = 12


def roll(x, shift, axis):
    return pltpu.roll(x, shift % x.shape[axis], axis)


def kernel(
    e_hbm, h_hbm, material, eps, bloch, orders,
    e_out, h_out, amp_out,
    fields, packed, from_left, from_right, turn, wave_x, wave_y, pick_n, want_m, split_a,
    parts, got_parts, pieces, got_pieces,
    load_sem, store_sem, halo_send, halo_recv, part_send, part_recv, piece_send, piece_recv,
):
    gx = lax.axis_index("gx")
    gy = lax.axis_index("gy")
    ring = gx % RING
    half = gx // RING
    place = half * GY + gy

    def device(dx, dy):
        return ((gx + dx + GX) % GX, (gy + dy + GY) % GY)

    def plane_device(index):
        return ((index // GY) * RING + ring, index % GY)

    def ring_device(index):
        return (half * RING + index, gy)

    barrier = pltpu.get_barrier_semaphore()
    around = [(1, 0), (-1, 0), (0, 1), (0, -1), (1, 1), (1, -1), (-1, 1), (-1, -1)]
    for dx, dy in around:
        pl.semaphore_signal(barrier, inc=1, device_id=device(dx, dy), device_id_type=MESH)

    @pl.loop(1, PLANE)
    def _(d):
        pl.semaphore_signal(barrier, inc=1, device_id=plane_device((place + d) % PLANE), device_id_type=MESH)

    @pl.loop(1, RING)
    def _(d):
        pl.semaphore_signal(barrier, inc=1, device_id=ring_device((ring + d) % RING), device_id_type=MESH)

    load_e = pltpu.make_async_copy(e_hbm, fields.at[0:6, 1 : Z + 1, 0], load_sem.at[0])
    load_h = pltpu.make_async_copy(h_hbm, fields.at[6:12, 1 : Z + 1, 0], load_sem.at[1])
    load_e.start()
    load_h.start()

    sub = lax.broadcasted_iota(jnp.int32, (8, 128), 0)
    lane = lax.broadcasted_iota(jnp.int32, (8, 128), 1)

    for c in range(6):
        fields[c, Z + 1] = jnp.zeros((4, 8, 128), F32)
        fields[6 + c, 0] = jnp.zeros((4, 8, 128), F32)

    @pl.loop(0, Z)
    def _(z):
        level = material[z]
        eps_cells = jnp.zeros((8, 128), F32)
        for k in range(8):
            eps_cells = jnp.where(level == k, eps[k], eps_cells)
        fields[COEF, z + 1, 0] = 0.5 / eps_cells

    load_e.wait()
    load_h.wait()

    @pl.loop(0, Z)
    def _(z):
        total = jnp.zeros((8, 128), F32)
        for c in range(13):
            total = jnp.where(lane // 8 == c, roll(fields[c, z + 1, 0], 8 * c + 4, 1), total)
        packed[z] = total

    pl.semaphore_wait(barrier, len(around) + PLANE - 1 + RING - 1)

    halos = []
    for part, (lo, hi) in enumerate(((TOP, Z), (0, TOP))):
        zs = slice(lo, hi)
        fz = slice(lo + 1, hi + 1)
        low, high = slice(0, 4), slice(4, 8)
        plan = [
            (fields.at[:, fz, 0, high], fields.at[:, fz, 2, high], (1, 0)),
            (fields.at[:, fz, 0, low], fields.at[:, fz, 2, low], (-1, 0)),
            (packed.at[zs], from_left.at[zs, 0], (0, 1)),
            (packed.at[zs], from_right.at[zs, 0], (0, -1)),
            (packed.at[zs, high], from_left.at[zs, 1, high], (1, 1)),
            (packed.at[zs, low], from_left.at[zs, 1, low], (-1, 1)),
            (packed.at[zs, high], from_right.at[zs, 1, high], (1, -1)),
            (packed.at[zs, low], from_right.at[zs, 1, low], (-1, -1)),
        ]
        copies = []
        for k, (src, dst, to) in enumerate(plan):
            copies.append(
                pltpu.make_async_remote_copy(
                    src_ref=src, dst_ref=dst, send_sem=halo_send.at[part, k], recv_sem=halo_recv.at[part, k],
                    device_id=device(*to), device_id_type=MESH,
                )
            )
        halos.append(copies)
    for copies in halos:
        for copy in copies:
            copy.start()

    phase_x = bloch[0]
    phase_y = bloch[1]

    ahead_x = jnp.where(gx == GX - 1, phase_x, 0.0)
    behind_x = jnp.where(gx == 0, -phase_x, 0.0)
    ahead_y = jnp.where(gy == GY - 1, phase_y, 0.0)
    behind_y = jnp.where(gy == 0, -phase_y, 0.0)
    turn_x = jnp.where(sub < 4, ahead_x, behind_x)
    turn_y = jnp.where(lane < 64, ahead_y, behind_y)
    for k, angle in enumerate((turn_y, turn_x, turn_x + turn_y)):
        turn[k, 0] = jnp.cos(angle)
        turn[k, 1] = jnp.sin(angle)

    m = lax.broadcasted_iota(jnp.int32, (SPAN, 128), 0) - SPAN // 2
    lanes = lax.broadcasted_iota(jnp.int32, (SPAN, 128), 1)
    along = gx * CX + lanes % CX
    angle = 2.0 * math.pi * ((m * along) & (NX - 1)).astype(F32) / NX + phase_x * along.astype(F32) / NX
    wave_x[...] = jnp.where(lanes < CX, jnp.cos(angle), jnp.where(lanes < 2 * CX, jnp.sin(angle), 0.0))
    along = gy * CY + lanes
    angle = 2.0 * math.pi * ((m * along) & (NY - 1)).astype(F32) / NY + phase_y * along.astype(F32) / NY
    scale = 1.0 / math.sqrt(NX * NY)
    cos_y = jnp.cos(angle) * scale
    sin_y = jnp.sin(angle) * scale
    for k in range(3):
        wave_y[k * SPAN : (k + 1) * SPAN, 0:128] = cos_y
        wave_y[k * SPAN : (k + 1) * SPAN, 128:256] = sin_y

    row16 = lax.broadcasted_iota(jnp.int32, (RING, 128), 0)
    lane16 = lax.broadcasted_iota(jnp.int32, (RING, 128), 1)
    diagonal16 = lane16 // 8 == row16
    by_owner = []
    for which in (0, 1):
        for x_half in range(HALVES):
            rows = [
                orders[which : which + 1, (x_half * RING + r) * 128 : (x_half * RING + r + 1) * 128]
                for r in range(RING)
            ]
            block = jnp.concatenate(rows, 0)
            total = jnp.zeros((RING, 128), jnp.int32)
            for k in range(RING):
                total = total + roll(jnp.where(diagonal16, roll(block, 8 * k, 1), 0), RING - k, 0)
            by_owner.append(total + SPAN // 2)
    for x_half in range(HALVES):
        for r in range(RING):
            want_m[x_half * RING + r] = by_owner[x_half][r : r + 1]
            want_m[PLANE + x_half * RING + r] = by_owner[HALVES + x_half][r : r + 1]

    n = lax.broadcasted_iota(jnp.int32, (SPAN, 128), 0)

    @pl.loop(0, PLANE)
    def _(t):
        hit = jnp.where(n == want_m[PLANE + t], 1.0, 0.0).astype(jnp.bfloat16)
        pick_n[t] = jnp.concatenate([hit, hit, hit], 0)

    def unpack(z):
        for rows in (0, 1):
            both = jnp.where(lane % 8 < 4, from_left[z, rows], from_right[z, rows])
            for c in range(13):
                fields[c, z + 1, 2 * rows + 1] = roll(both, 128 - (8 * c + 4), 1)
        for c in (0, 1, 2, 6, 7, 8):
            for k in range(3):
                re = fields[c, z + 1, k + 1]
                im = fields[c + 3, z + 1, k + 1]
                fields[c, z + 1, k + 1] = turn[k, 0] * re - turn[k, 1] * im
                fields[c + 3, z + 1, k + 1] = turn[k, 1] * re + turn[k, 0] * im

    first_sub, last_sub = sub == 0, sub == 7
    first_lane, last_lane = lane == 0, lane == 127

    def tiles(slot, z):
        return [fields[slot, z, k] for k in range(4)]

    def shifted(t, shift, axis, seam):
        step = 2 if axis == 0 else 1
        r = [roll(v, shift, axis) for v in t]
        return [jnp.where(seam, r[k ^ step], r[k]) for k in range(4)]

    def update_h(z):
        for p in (0, 3):
            x, y, w = (tiles(p + c, z) for c in range(3))
            x_up, y_up = (tiles(p + c, z + 1) for c in range(2))
            y_ax = shifted(y, -1, 0, last_sub)
            w_ax = shifted(w, -1, 0, last_sub)
            x_ay = shifted(x, -1, 1, last_lane)
            w_ay = shifted(w, -1, 1, last_lane)
            for k in range(4):
                cx = w_ay[k] - w[k] - (y_up[k] - y[k])
                cy = x_up[k] - x[k] - (w_ax[k] - w[k])
                cz = y_ax[k] - y[k] - (x_ay[k] - x[k])
                for c, curl in enumerate((cx, cy, cz)):
                    fields[6 + p + c, z, k] = fields[6 + p + c, z, k] - 0.5 * curl

    def update_e(z):
        coef = tiles(COEF, z)
        for p in (0, 3):
            x, y, w = (tiles(6 + p + c, z) for c in range(3))
            x_dn, y_dn = (tiles(6 + p + c, z - 1) for c in range(2))
            y_bx = shifted(y, 1, 0, first_sub)
            w_bx = shifted(w, 1, 0, first_sub)
            x_by = shifted(x, 1, 1, first_lane)
            w_by = shifted(w, 1, 1, first_lane)
            for k in range(4):
                cx = w[k] - w_by[k] - (y[k] - y_dn[k])
                cy = x[k] - x_dn[k] - (w[k] - w_bx[k])
                cz = y[k] - y_bx[k] - (x[k] - x_by[k])
                for c, curl in enumerate((cx, cy, cz)):
                    fields[p + c, z, k] = fields[p + c, z, k] + coef[k] * curl

    def over(lo, hi, body):
        @pl.loop(lo, hi)
        def _(z):
            body(z)

    for copy in halos[0]:
        copy.wait()
    over(TOP, Z, unpack)
    for s in range(STEPS):
        over(TOP + s + 1, Z + 1, update_h)
        over(TOP + s + 2, Z + 1, update_e)

    flat = []
    for c in (0, 1):
        re = fields[c, Z - 1, 0]
        im = fields[c + 3, Z - 1, 0]
        flat.append(jnp.concatenate([re, im], 0))
        flat.append(jnp.concatenate([im, -re], 0))
    plane = jnp.concatenate(flat, 1)
    sums = jnp.dot(wave_x[:, 0 : 2 * CX], plane, precision=lax.Precision.HIGHEST, preferred_element_type=F32)
    re0, im0, re1, im1 = (sums[:, k * 128 : (k + 1) * 128] for k in range(4))
    left = jnp.concatenate(
        [
            jnp.concatenate([re0, re1, im0, im1], 0),
            jnp.concatenate([im0, im1, -re0, -re1], 0),
        ],
        1,
    )
    table = lax.dot_general(
        left, wave_y[...], (((1,), (1,)), ((), ())), precision=lax.Precision.HIGHEST, preferred_element_type=F32
    )
    high = table.astype(jnp.bfloat16).astype(F32)
    rest = table - high
    middle = rest.astype(jnp.bfloat16).astype(F32)
    low = rest - middle
    column = lax.broadcasted_iota(jnp.int32, table.shape, 1)
    split_a[...] = jnp.where(column < SPAN, high, jnp.where(column < 2 * SPAN, middle, low)).astype(jnp.bfloat16)

    @pl.loop(0, PLANE)
    def _(d):
        t = (place + d) % PLANE
        by_m = jnp.dot(split_a[...], pick_n[t], preferred_element_type=F32)
        hit = n == want_m[t]
        found = [
            jnp.sum(jnp.where(hit, by_m[r * SPAN : (r + 1) * SPAN], 0.0), 0, keepdims=True) for r in (0, 2, 1, 3)
        ]
        parts[t] = jnp.concatenate(found, 0)

        @pl.when(d != 0)
        def _():
            pltpu.make_async_remote_copy(
                src_ref=parts.at[t], dst_ref=got_parts.at[place], send_sem=part_send, recv_sem=part_recv,
                device_id=plane_device(t), device_id_type=MESH,
            ).start()

    got_parts[place] = parts[place]
    pltpu.make_async_copy(got_parts.at[0 : PLANE - 1], got_parts.at[0 : PLANE - 1], part_recv).wait()
    mine = jnp.sum(got_parts[...], 0)

    tall = jnp.concatenate([mine, jnp.zeros((RING - 4, 128), F32)], 0)
    rows = jnp.zeros((RING, 128), F32)
    for k in range(RING):
        rows = rows + roll(jnp.where(diagonal16, roll(tall, 8 * k, 1), 0.0), RING - k, 0)
    for r in range(RING):
        pieces[r] = rows[r : r + 1]

    @pl.loop(1, RING)
    def _(d):
        to = (ring + d) % RING
        pltpu.make_async_remote_copy(
            src_ref=pieces.at[to], dst_ref=got_pieces.at[ring], send_sem=piece_send, recv_sem=piece_recv,
            device_id=ring_device(to), device_id_type=MESH,
        ).start()

    got_pieces[ring] = pieces[ring]

    for copy in halos[1]:
        copy.wait()
    over(0, TOP, unpack)
    for s in range(STEPS):
        over(1, TOP + s + 1, update_h)
        over(1, TOP + s + 2, update_e)
    store_e = pltpu.make_async_copy(fields.at[0:6, 1 : Z + 1, 0], e_out, store_sem.at[0])
    store_h = pltpu.make_async_copy(fields.at[6:12, 1 : Z + 1, 0], h_out, store_sem.at[1])
    store_e.start()
    store_h.start()

    pltpu.make_async_copy(got_pieces.at[0 : RING - 1], got_pieces.at[0 : RING - 1], piece_recv).wait()
    amp_out[...] = jnp.sum(got_pieces[...], 0)

    pltpu.make_async_copy(parts.at[0 : PLANE - 1], parts.at[0 : PLANE - 1], part_send).wait()
    pltpu.make_async_copy(pieces.at[0 : RING - 1], pieces.at[0 : RING - 1], piece_send).wait()
    store_e.wait()
    store_h.wait()


def per_device(e_field, h_field, material, eps_table, bloch_phase, orders):
    vmem = pl.BlockSpec(memory_space=pltpu.VMEM)
    smem = pl.BlockSpec(memory_space=pltpu.SMEM)
    hbm = pl.BlockSpec(memory_space=pl.ANY)
    e_next, h_next, amplitudes = pl.pallas_call(
        kernel,
        out_shape=(
            jax.ShapeDtypeStruct(e_field.shape, F32),
            jax.ShapeDtypeStruct(h_field.shape, F32),
            jax.ShapeDtypeStruct((1, 128), F32),
        ),
        in_specs=[hbm, hbm, vmem, smem, smem, vmem],
        out_specs=(hbm, hbm, vmem),
        scratch_shapes=[
            pltpu.VMEM((13, Z + 2, 4, 8, 128), F32),
            pltpu.VMEM((Z, 8, 128), F32),
            pltpu.VMEM((Z, 2, 8, 128), F32),
            pltpu.VMEM((Z, 2, 8, 128), F32),
            pltpu.VMEM((3, 2, 8, 128), F32),
            pltpu.VMEM((SPAN, 128), F32),
            pltpu.VMEM((3 * SPAN, 256), F32),
            pltpu.VMEM((PLANE, 3 * SPAN, 128), jnp.bfloat16),
            pltpu.VMEM((2 * PLANE, 1, 128), jnp.int32),
            pltpu.VMEM((4 * SPAN, 3 * SPAN), jnp.bfloat16),
            pltpu.VMEM((PLANE, 4, 128), F32),
            pltpu.VMEM((PLANE, 4, 128), F32),
            pltpu.VMEM((RING, 1, 128), F32),
            pltpu.VMEM((RING, 1, 128), F32),
            pltpu.SemaphoreType.DMA((2,)),
            pltpu.SemaphoreType.DMA((2,)),
            pltpu.SemaphoreType.DMA((2, 8)),
            pltpu.SemaphoreType.DMA((2, 8)),
            pltpu.SemaphoreType.DMA,
            pltpu.SemaphoreType.DMA,
            pltpu.SemaphoreType.DMA,
            pltpu.SemaphoreType.DMA,
        ],
        compiler_params=pltpu.CompilerParams(
            collective_id=0, has_side_effects=True, vmem_limit_bytes=32 * 2**20
        ),
    )(e_field, h_field, material, eps_table, bloch_phase, orders)
    return e_next, h_next, amplitudes[0, :32].reshape(4, 8)


def solution(mesh):
    return jax.shard_map(
        per_device,
        mesh=mesh,
        in_specs=(
            P(None, None, "gx", "gy"),
            P(None, None, "gx", "gy"),
            P(None, "gx", "gy"),
            P(),
            P(),
            P(),
        ),
        out_specs=(P(None, None, "gx", "gy"), P(None, None, "gx", "gy"), P(None, ("gx", "gy"))),
        check_vma=False,
    )
```

```python
import math

import jax
import jax.numpy as jnp
from jax import lax
from jax.experimental import pallas as pl
from jax.experimental.pallas import tpu as pltpu
from jax.sharding import PartitionSpec as P

MESH = pl.DeviceIdType.MESH
F32 = jnp.float32

STEPS = 4
Z = 20
NX = 256
NY = 2048
GX = 32
GY = 16
RING = 16
HALVES = GX // RING
PLANE = HALVES * GY
CX = NX // GX
CY = NY // GY
SPAN = 64
GROUPS = ((14, 20), (6, 14), (0, 6))
TOP = 14
WIDE = 4
WIDTH = 6
COEF = 12


def roll(x, shift, axis):
    return pltpu.roll(x, shift % x.shape[axis], axis)


def kernel(
    e_hbm, h_hbm, material_hbm, eps_hbm, bloch_hbm, orders_hbm,
    e_out, h_out, amp_out,
    fields, material, orders, eps, bloch, packed, from_left, from_right, turn, own, own_coef, edge_coef, coef_left, coef_right, wave_x, wave_y, pick_n, want, split_a,
    parts, got_parts, pieces, got_pieces,
    load_sem, store_sem, coef_send, coef_recv, halo_send, halo_recv, part_send, part_recv, piece_send, piece_recv,
):
    gx = lax.axis_index("gx")
    gy = lax.axis_index("gy")
    ring = gx % RING
    half = gx // RING
    place = half * GY + gy

    def device(dx, dy):
        return ((gx + dx + GX) % GX, (gy + dy + GY) % GY)

    def plane_device(index):
        return ((index // GY) * RING + ring, index % GY)

    def ring_device(index):
        return (half * RING + index, gy)

    barrier = pltpu.get_barrier_semaphore()
    around = [(1, 0), (-1, 0), (0, 1), (0, -1), (1, 1), (1, -1), (-1, 1), (-1, -1)]

    @pl.loop(1, RING)
    def _(d):
        pl.semaphore_signal(barrier, inc=1, device_id=ring_device((ring + d) % RING), device_id_type=MESH)

    for dx, dy in around:
        pl.semaphore_signal(barrier, inc=1, device_id=device(dx, dy), device_id_type=MESH)

    @pl.loop(1, PLANE)
    def _(d):
        pl.semaphore_signal(barrier, inc=1, device_id=plane_device((place + d) % PLANE), device_id_type=MESH)

    loads = [
        pltpu.make_async_copy(src, dst, load_sem.at[k])
        for k, (src, dst) in enumerate(
            (
                (material_hbm, material),
                (eps_hbm, eps),
                (bloch_hbm, bloch),
                (e_hbm, fields.at[0:6, 1 : Z + 1, 0]),
                (h_hbm, fields.at[6:12, 1 : Z + 1, 0]),
                (orders_hbm, orders),
                (e_hbm.at[:, TOP:Z], own.at[0:6, 0 : Z - TOP, 0]),
                (h_hbm.at[:, TOP:Z], own.at[6:12, 0 : Z - TOP, 0]),
            )
        )
    ]
    for load in loads:
        load.start()

    sub = lax.broadcasted_iota(jnp.int32, (8, 128), 0)
    lane = lax.broadcasted_iota(jnp.int32, (8, 128), 1)

    for c in range(6):
        fields[c, Z + 1] = jnp.zeros((4, 8, 128), F32)
        fields[6 + c, 0] = jnp.zeros((4, 8, 128), F32)
        own[c, Z - TOP] = jnp.zeros((4, 8, 128), F32)
    for c in range(12):
        for z in range(Z - TOP):
            own[c, z, 1:4] = jnp.zeros((3, 8, 128), F32)

    for load in loads[0:3]:
        load.wait()

    @pl.loop(0, Z // 5)
    def _(k):
        for i in range(5):
            z = 5 * k + i
            level = material[z]
            eps_cells = jnp.zeros((8, 128), F32)
            for n in range(8):
                eps_cells = jnp.where(level == n, eps[n], eps_cells)
            fields[COEF, z + 1, 0] = 0.5 / eps_cells

    total = jnp.zeros((8, 128), F32)
    for z in range(Z - TOP):
        tile = fields[COEF, TOP + z + 1, 0]
        own_coef[z, 0] = tile
        total = jnp.where(lane // 8 == z, roll(tile, 8 * z + 4, 1), total)
    edge_coef[...] = total

    pl.semaphore_wait(barrier, len(around) + PLANE - 1 + RING - 1)

    low, high = slice(0, 4), slice(4, 8)
    near = []
    for k, (src, dst, to) in enumerate(
        (
            (own_coef.at[:, 0, high], own_coef.at[:, 2, high], (1, 0)),
            (own_coef.at[:, 0, low], own_coef.at[:, 2, low], (-1, 0)),
            (edge_coef, coef_left.at[0], (0, 1)),
            (edge_coef, coef_right.at[0], (0, -1)),
            (edge_coef.at[high], coef_left.at[1, high], (1, 1)),
            (edge_coef.at[low], coef_left.at[1, low], (-1, 1)),
            (edge_coef.at[high], coef_right.at[1, high], (1, -1)),
            (edge_coef.at[low], coef_right.at[1, low], (-1, -1)),
        )
    ):
        near.append(
            pltpu.make_async_remote_copy(
                src_ref=src, dst_ref=dst, send_sem=coef_send.at[k], recv_sem=coef_recv.at[k],
                device_id=device(*to), device_id_type=MESH,
            )
        )
        near[-1].start()

    for load in loads[3:5]:
        load.wait()

    halos = []
    for part, (lo, hi) in enumerate(GROUPS):
        zs = slice(lo // 2, hi // 2)
        fz = slice(lo + 1, hi + 1)
        plan = [
            (fields.at[:, fz, 0, high], fields.at[:, fz, 2, high], (1, 0)),
            (fields.at[:, fz, 0, low], fields.at[:, fz, 2, low], (-1, 0)),
            (packed.at[0, zs], from_left.at[zs, 0], (0, 1)),
            (packed.at[1, zs], from_right.at[zs, 0], (0, -1)),
            (packed.at[0, zs, high], from_left.at[zs, 1, high], (1, 1)),
            (packed.at[0, zs, low], from_left.at[zs, 1, low], (-1, 1)),
            (packed.at[1, zs, high], from_right.at[zs, 1, high], (1, -1)),
            (packed.at[1, zs, low], from_right.at[zs, 1, low], (-1, -1)),
        ]
        copies = []
        for k, (src, dst, to) in enumerate(plan):
            copies.append(
                pltpu.make_async_remote_copy(
                    src_ref=src, dst_ref=dst, send_sem=halo_send.at[part, k], recv_sem=halo_recv.at[part, k],
                    device_id=device(*to), device_id_type=MESH,
                )
            )
        halos.append(copies)
    for copies in halos:
        for copy in copies[:2]:
            copy.start()

    even = lane % 8 < 4

    @pl.loop(0, Z // 4)
    def _(k):
        for i in (0, 1):
            pair = []
            for z in (4 * k + 2 * i, 4 * k + 2 * i + 1):
                total = jnp.zeros((8, 128), F32)
                for c in range(13):
                    total = jnp.where(lane // 8 == c, roll(fields[c, z + 1, 0], 8 * c + 4, 1), total)
                pair.append(total)
            packed[0, 2 * k + i] = jnp.where(even, pair[0], roll(pair[1], 4, 1))
            packed[1, 2 * k + i] = jnp.where(even, roll(pair[0], -4, 1), pair[1])

    for copies in halos:
        for copy in copies[2:]:
            copy.start()

    phase_x = bloch[0]
    phase_y = bloch[1]

    ahead_x = jnp.where(gx == GX - 1, phase_x, 0.0)
    behind_x = jnp.where(gx == 0, -phase_x, 0.0)
    ahead_y = jnp.where(gy == GY - 1, phase_y, 0.0)
    behind_y = jnp.where(gy == 0, -phase_y, 0.0)
    turn_x = jnp.where(sub < 4, ahead_x, behind_x)
    turn_y = jnp.where(lane < 64, ahead_y, behind_y)
    for k, angle in enumerate((turn_y, turn_x, turn_x + turn_y)):
        turn[k, 0] = jnp.cos(angle)
        turn[k, 1] = jnp.sin(angle)

    m = lax.broadcasted_iota(jnp.int32, (SPAN, 128), 0) - SPAN // 2
    lanes = lax.broadcasted_iota(jnp.int32, (SPAN, 128), 1)
    along = lanes % 16
    along = gx * CX + jnp.where(along < 12, along, along - 16)
    angle = 2.0 * math.pi * ((m * along) & (NX - 1)).astype(F32) / NX + phase_x * along.astype(F32) / NX
    wave_x[...] = jnp.where(lanes < 16, jnp.cos(angle), jnp.where(lanes < 32, jnp.sin(angle), 0.0))
    scale = 1.0 / math.sqrt(NX * NY)
    for k, (offset, valid) in enumerate(((lanes, None), (jnp.where(lanes < 64, lanes + CY, lanes - 128), (lanes < 4) | (lanes >= 124)))):
        along = gy * CY + offset
        angle = 2.0 * math.pi * ((m * along) & (NY - 1)).astype(F32) / NY + phase_y * along.astype(F32) / NY
        cos_y = jnp.cos(angle) * scale
        sin_y = jnp.sin(angle) * scale
        if valid is not None:
            cos_y = jnp.where(valid, cos_y, 0.0)
            sin_y = jnp.where(valid, sin_y, 0.0)
        for i in range(3):
            wave_y[i * SPAN : (i + 1) * SPAN, k * 128 : (k + 1) * 128] = cos_y
            wave_y[i * SPAN : (i + 1) * SPAN, 256 + k * 128 : 256 + (k + 1) * 128] = sin_y

    loads[5].wait()
    row16 = lax.broadcasted_iota(jnp.int32, (RING, 128), 0)
    lane16 = lax.broadcasted_iota(jnp.int32, (RING, 128), 1)
    diagonal16 = lane16 // 8 == row16
    by_owner = []
    for which in (0, 1):
        for x_half in range(HALVES):
            rows = [
                orders[which : which + 1, (x_half * RING + r) * 128 : (x_half * RING + r + 1) * 128]
                for r in range(RING)
            ]
            block = jnp.concatenate(rows, 0)
            total = jnp.zeros((RING, 128), jnp.int32)
            for k in range(RING):
                total = total + roll(jnp.where(diagonal16, roll(block, 8 * k, 1), 0), RING - k, 0)
            by_owner.append(total + SPAN // 2)
    for t in range(PLANE):
        x_half, r = divmod(t, RING)
        at = slice(t % WIDE * 128, (t % WIDE + 1) * 128)
        want[0, t // WIDE, :, at] = by_owner[x_half][r : r + 1]
        want[1, t // WIDE, :, at] = by_owner[HALVES + x_half][r : r + 1]

    n = lax.broadcasted_iota(jnp.int32, (SPAN, WIDE * 128), 0)

    @pl.loop(0, PLANE // WIDE)
    def _(t):
        hit = jnp.where(n == want[1, t], 1.0, 0.0).astype(jnp.bfloat16)
        for k in range(3):
            pick_n[t, k * SPAN : (k + 1) * SPAN] = hit

    def unpack(pair):
        for rows in (0, 1):
            left, right = from_left[pair, rows], from_right[pair, rows]
            for i, both in enumerate(
                (jnp.where(even, left, roll(right, 4, 1)), jnp.where(even, roll(left, -4, 1), right))
            ):
                for c in range(13):
                    fields[c, 2 * pair + i + 1, 2 * rows + 1] = roll(both, -(8 * c + 4), 1)
        for z in (2 * pair, 2 * pair + 1):
            turn_halo(z)

    def turn_halo(z):
        for c in (0, 1, 2, 6, 7, 8):
            for k in range(3):
                re = fields[c, z + 1, k + 1]
                im = fields[c + 3, z + 1, k + 1]
                fields[c, z + 1, k + 1] = turn[k, 0] * re - turn[k, 1] * im
                fields[c + 3, z + 1, k + 1] = turn[k, 1] * re + turn[k, 0] * im

    first_sub, last_sub = sub == 0, sub == 7
    first_lane, last_lane = lane == 0, lane == 127

    def shifted(t, shift, axis, seam):
        step = 2 if axis == 0 else 1
        r = [roll(v, shift, axis) for v in t]
        return [jnp.where(seam, r[k ^ step], r[k]) for k in range(4)]

    def updates(held, coef_of):
        def tiles(slot, z):
            return [held[slot, z, k] for k in range(4)]

        def update_h(z):
            for p in (0, 3):
                x, y, w = (tiles(p + c, z) for c in range(3))
                x_up, y_up = (tiles(p + c, z + 1) for c in range(2))
                y_ax = shifted(y, -1, 0, last_sub)
                w_ax = shifted(w, -1, 0, last_sub)
                x_ay = shifted(x, -1, 1, last_lane)
                w_ay = shifted(w, -1, 1, last_lane)
                for k in range(4):
                    cx = w_ay[k] - w[k] - (y_up[k] - y[k])
                    cy = x_up[k] - x[k] - (w_ax[k] - w[k])
                    cz = y_ax[k] - y[k] - (x_ay[k] - x[k])
                    for c, curl in enumerate((cx, cy, cz)):
                        held[6 + p + c, z, k] = held[6 + p + c, z, k] - 0.5 * curl

        def update_e(z):
            coef = [coef_of(z, k) for k in range(4)]
            for p in (0, 3):
                x, y, w = (tiles(6 + p + c, z) for c in range(3))
                x_dn, y_dn = (tiles(6 + p + c, z - 1) for c in range(2))
                y_bx = shifted(y, 1, 0, first_sub)
                w_bx = shifted(w, 1, 0, first_sub)
                x_by = shifted(x, 1, 1, first_lane)
                w_by = shifted(w, 1, 1, first_lane)
                for k in range(4):
                    cx = w[k] - w_by[k] - (y[k] - y_dn[k])
                    cy = x[k] - x_dn[k] - (w[k] - w_bx[k])
                    cz = y[k] - y_bx[k] - (x[k] - x_by[k])
                    for c, curl in enumerate((cx, cy, cz)):
                        held[p + c, z, k] = held[p + c, z, k] + coef[k] * curl

        return update_h, update_e

    update_h, update_e = updates(fields, lambda z, k: fields[COEF, z, k])
    own_h, own_e = updates(own, lambda z, k: own_coef[z, k])

    def over(lo, hi, body, width):
        chunks = (hi - lo) // width

        @pl.loop(0, chunks)
        def _(k):
            for i in range(width):
                body(lo + k * width + i)

        for z in range(lo + chunks * width, hi):
            body(z)

    def advance(group):
        lo, hi = GROUPS[group]
        for copy in halos[group]:
            copy.wait()
        over(lo // 2, hi // 2, unpack, 1)
        for s in range(STEPS):
            above = Z if hi == Z else hi + s
            over((lo + s if lo else 0) + 1, above + 1, update_h, WIDTH)
            above = Z if hi == Z else hi + s + 1
            over((lo + s + 1 if lo else 0) + 1, above + 1, update_e, WIDTH)

    for copy in near:
        copy.wait()
    for rows in (0, 1):
        both = jnp.where(even, coef_left[rows], coef_right[rows])
        for z in range(Z - TOP):
            own_coef[z, 2 * rows + 1] = roll(both, -(8 * z + 4), 1)
    for load in loads[6:8]:
        load.wait()
    for s in range(STEPS):
        for z in range(s, Z - TOP if s < STEPS - 1 else Z - TOP - 1):
            own_h(z)
        for z in range(s + 1, Z - TOP if s < STEPS - 1 else Z - TOP - 1):
            own_e(z)

    flat = []
    at = Z - 2 - TOP
    for c in (0, 1):
        re = [own[c, at, k] for k in range(4)]
        im = [own[c + 3, at, k] for k in range(4)]
        for k in (0, 1):
            flat.append(jnp.concatenate([re[k], re[k + 2], im[k], im[k + 2]], 0))
        for k in (0, 1):
            flat.append(jnp.concatenate([im[k], im[k + 2], -re[k], -re[k + 2]], 0))
    plane = jnp.concatenate(flat, 1)
    sums = jnp.dot(wave_x[:, 0:32], plane, precision=lax.Precision.HIGHEST, preferred_element_type=F32)
    re0, im0, re1, im1 = (sums[:, k * 256 : (k + 1) * 256] for k in range(4))
    left = jnp.concatenate(
        [
            jnp.concatenate([re0, re1, im0, im1], 0),
            jnp.concatenate([im0, im1, -re0, -re1], 0),
        ],
        1,
    )
    table = lax.dot_general(
        left, wave_y[...], (((1,), (1,)), ((), ())), precision=lax.Precision.HIGHEST, preferred_element_type=F32
    )
    high = table.astype(jnp.bfloat16).astype(F32)
    rest = table - high
    middle = rest.astype(jnp.bfloat16).astype(F32)
    low = rest - middle
    column = lax.broadcasted_iota(jnp.int32, table.shape, 1)
    split_a[...] = jnp.where(column < SPAN, high, jnp.where(column < 2 * SPAN, middle, low)).astype(jnp.bfloat16)

    @pl.loop(0, PLANE // WIDE)
    def _(d):
        t = (place // WIDE + d) % (PLANE // WIDE)
        by_m = jnp.dot(split_a[...], pick_n[t], preferred_element_type=F32)
        hit = n == want[0, t]
        found = [
            jnp.sum(jnp.where(hit, by_m[r * SPAN : (r + 1) * SPAN], 0.0), 0, keepdims=True) for r in (0, 2, 1, 3)
        ]
        found = jnp.concatenate(found, 0)
        for k in range(WIDE):
            parts[t * WIDE + k] = found[:, k * 128 : (k + 1) * 128]
        for k in range(WIDE):
            to = t * WIDE + k

            @pl.when(to != place)
            def _():
                pltpu.make_async_remote_copy(
                    src_ref=parts.at[to], dst_ref=got_parts.at[place], send_sem=part_send, recv_sem=part_recv,
                    device_id=plane_device(to), device_id_type=MESH,
                ).start()

    advance(0)
    got_parts[place] = parts[place]
    pltpu.make_async_copy(got_parts.at[0 : PLANE - 1], got_parts.at[0 : PLANE - 1], part_recv).wait()
    mine = jnp.sum(got_parts[...], 0)

    tall = jnp.concatenate([mine, jnp.zeros((RING - 4, 128), F32)], 0)
    rows = jnp.zeros((RING, 128), F32)
    for k in range(RING):
        rows = rows + roll(jnp.where(diagonal16, roll(tall, 8 * k, 1), 0.0), RING - k, 0)
    for r in range(RING):
        pieces[r] = rows[r : r + 1]

    @pl.loop(1, RING)
    def _(d):
        to = (ring + d) % RING
        pltpu.make_async_remote_copy(
            src_ref=pieces.at[to], dst_ref=got_pieces.at[ring], send_sem=piece_send, recv_sem=piece_recv,
            device_id=ring_device(to), device_id_type=MESH,
        ).start()

    got_pieces[ring] = pieces[ring]

    advance(1)
    advance(2)
    store_e = pltpu.make_async_copy(fields.at[0:6, 1 : Z + 1, 0], e_out, store_sem.at[0])
    store_h = pltpu.make_async_copy(fields.at[6:12, 1 : Z + 1, 0], h_out, store_sem.at[1])
    store_e.start()
    store_h.start()

    pltpu.make_async_copy(got_pieces.at[0 : RING - 1], got_pieces.at[0 : RING - 1], piece_recv).wait()
    total = jnp.broadcast_to(jnp.sum(got_pieces[...], 0), (8, 128))
    rows = total
    for r in range(1, 4):
        rows = jnp.where(sub == r, roll(total, -8 * r, 1), rows)
    amp_out[...] = rows

    pltpu.make_async_copy(parts.at[0 : PLANE - 1], parts.at[0 : PLANE - 1], part_send).wait()
    pltpu.make_async_copy(pieces.at[0 : RING - 1], pieces.at[0 : RING - 1], piece_send).wait()
    store_e.wait()
    store_h.wait()


def hand_over(e_in, h_in, amp_in, e_out, h_out, amp_out, held, in_sems, out_sems):
    ends = [(e_in, e_out, c) for c in range(6)] + [(h_in, h_out, c) for c in range(6)]
    loads = [pltpu.make_async_copy(src.at[c], held.at[k], in_sems.at[k]) for k, (src, _, c) in enumerate(ends)]
    stores = [pltpu.make_async_copy(held.at[k], dst.at[c], out_sems.at[k]) for k, (_, dst, c) in enumerate(ends)]
    for load in loads:
        load.start()
    amp_out[...] = amp_in[0:4, 0:8]
    for load, store in zip(loads, stores):
        load.wait()
        store.start()
    for store in stores:
        store.wait()


def per_device(e_field, h_field, material, eps_table, bloch_phase, orders):
    vmem = pl.BlockSpec(memory_space=pltpu.VMEM)
    hbm = pl.BlockSpec(memory_space=pltpu.HBM)
    e_next, h_next, amplitudes = pl.pallas_call(
        kernel,
        out_shape=(
            jax.ShapeDtypeStruct(e_field.shape, F32),
            jax.ShapeDtypeStruct(h_field.shape, F32),
            jax.ShapeDtypeStruct((8, 128), F32),
        ),
        in_specs=[hbm] * 6,
        out_specs=(hbm, hbm, vmem),
        scratch_shapes=[
            pltpu.VMEM((13, Z + 2, 4, 8, 128), F32),
            pltpu.VMEM((Z, 8, 128), jnp.int32),
            pltpu.VMEM((2, 4096), jnp.int32),
            pltpu.SMEM((8,), F32),
            pltpu.SMEM((2,), F32),
            pltpu.VMEM((2, Z // 2, 8, 128), F32),
            pltpu.VMEM((Z // 2, 2, 8, 128), F32),
            pltpu.VMEM((Z // 2, 2, 8, 128), F32),
            pltpu.VMEM((3, 2, 8, 128), F32),
            pltpu.VMEM((12, Z - TOP + 1, 4, 8, 128), F32),
            pltpu.VMEM((Z - TOP, 4, 8, 128), F32),
            pltpu.VMEM((8, 128), F32),
            pltpu.VMEM((2, 8, 128), F32),
            pltpu.VMEM((2, 8, 128), F32),
            pltpu.VMEM((SPAN, 128), F32),
            pltpu.VMEM((3 * SPAN, 512), F32),
            pltpu.VMEM((PLANE // WIDE, 3 * SPAN, WIDE * 128), jnp.bfloat16),
            pltpu.VMEM((2, PLANE // WIDE, 1, WIDE * 128), jnp.int32),
            pltpu.VMEM((4 * SPAN, 3 * SPAN), jnp.bfloat16),
            pltpu.VMEM((PLANE, 4, 128), F32),
            pltpu.VMEM((PLANE, 4, 128), F32),
            pltpu.VMEM((RING, 1, 128), F32),
            pltpu.VMEM((RING, 1, 128), F32),
            pltpu.SemaphoreType.DMA((8,)),
            pltpu.SemaphoreType.DMA((2,)),
            pltpu.SemaphoreType.DMA((8,)),
            pltpu.SemaphoreType.DMA((8,)),
            pltpu.SemaphoreType.DMA((len(GROUPS), 8)),
            pltpu.SemaphoreType.DMA((len(GROUPS), 8)),
            pltpu.SemaphoreType.DMA,
            pltpu.SemaphoreType.DMA,
            pltpu.SemaphoreType.DMA,
            pltpu.SemaphoreType.DMA,
        ],
        compiler_params=pltpu.CompilerParams(
            collective_id=0, has_side_effects=True, vmem_limit_bytes=60 * 2**20
        ),
    )(e_field, h_field, material, eps_table, bloch_phase, orders)
    return pl.pallas_call(
        hand_over,
        out_shape=(
            jax.ShapeDtypeStruct(e_field.shape, F32),
            jax.ShapeDtypeStruct(h_field.shape, F32),
            jax.ShapeDtypeStruct((4, 8), F32),
        ),
        in_specs=[hbm, hbm, vmem],
        out_specs=(hbm, hbm, vmem),
        scratch_shapes=[
            pltpu.VMEM((12,) + e_field.shape[1:], F32),
            pltpu.SemaphoreType.DMA((12,)),
            pltpu.SemaphoreType.DMA((12,)),
        ],
        compiler_params=pltpu.CompilerParams(vmem_limit_bytes=60 * 2**20),
    )(e_next, h_next, amplitudes)


def solution(mesh):
    return jax.shard_map(
        per_device,
        mesh=mesh,
        in_specs=(
            P(None, None, "gx", "gy"),
            P(None, None, "gx", "gy"),
            P(None, "gx", "gy"),
            P(),
            P(),
            P(),
        ),
        out_specs=(P(None, None, "gx", "gy"), P(None, None, "gx", "gy"), P(None, ("gx", "gy"))),
        check_vma=False,
    )
```

```python
import math

import jax
import jax.numpy as jnp
from jax import lax
from jax.experimental import pallas as pl
from jax.experimental.pallas import tpu as pltpu
from jax.sharding import PartitionSpec as P

MESH = pl.DeviceIdType.MESH
F32 = jnp.float32

STEPS = 4
Z = 20
NX = 256
NY = 2048
GX = 32
GY = 16
RING = 16
HALVES = GX // RING
PLANE = HALVES * GY
CX = NX // GX
CY = NY // GY
SPAN = 64
GROUPS = ((14, 20), (6, 14), (0, 6))
TOP = 14
WIDE = 4
WIDTH = 6
COEF = 12


def roll(x, shift, axis):
    return pltpu.roll(x, shift % x.shape[axis], axis)


def kernel(
    e_hbm, h_hbm, material_hbm, eps_hbm, bloch_hbm, orders_hbm,
    e_out, h_out, amp_out,
    fields, material, orders, eps, bloch, packed, from_left, from_right, turn, own, own_coef, edge_coef, coef_left, coef_right, wave_x, wave_y, pick_n, want, split_a,
    parts, got_parts, pieces, got_pieces,
    load_sem, store_sem, coef_send, coef_recv, halo_send, halo_recv, part_send, part_recv, piece_send, piece_recv,
):
    gx = lax.axis_index("gx")
    gy = lax.axis_index("gy")
    ring = gx % RING
    half = gx // RING
    place = half * GY + gy

    def device(dx, dy):
        return ((gx + dx + GX) % GX, (gy + dy + GY) % GY)

    def plane_device(index):
        return ((index // GY) * RING + ring, index % GY)

    def ring_device(index):
        return (half * RING + index, gy)

    barrier = pltpu.get_barrier_semaphore()
    around = [(1, 0), (-1, 0), (0, 1), (0, -1), (1, 1), (1, -1), (-1, 1), (-1, -1)]

    @pl.loop(1, RING)
    def _(d):
        pl.semaphore_signal(barrier, inc=1, device_id=ring_device((ring + d) % RING), device_id_type=MESH)

    for dx, dy in around:
        pl.semaphore_signal(barrier, inc=1, device_id=device(dx, dy), device_id_type=MESH)

    @pl.loop(1, PLANE)
    def _(d):
        pl.semaphore_signal(barrier, inc=1, device_id=plane_device((place + d) % PLANE), device_id_type=MESH)

    loads = [
        pltpu.make_async_copy(src, dst, load_sem.at[k])
        for k, (src, dst) in enumerate(
            (
                (material_hbm, material),
                (eps_hbm, eps),
                (bloch_hbm, bloch),
                (e_hbm, fields.at[0:6, 1 : Z + 1, 0]),
                (h_hbm, fields.at[6:12, 1 : Z + 1, 0]),
                (orders_hbm, orders),
                (e_hbm.at[:, TOP:Z], own.at[0:6, 0 : Z - TOP, 0]),
                (h_hbm.at[:, TOP:Z], own.at[6:12, 0 : Z - TOP, 0]),
            )
        )
    ]
    for load in loads:
        load.start()

    sub = lax.broadcasted_iota(jnp.int32, (8, 128), 0)
    lane = lax.broadcasted_iota(jnp.int32, (8, 128), 1)

    for c in range(6):
        fields[c, Z + 1] = jnp.zeros((4, 8, 128), F32)
        fields[6 + c, 0] = jnp.zeros((4, 8, 128), F32)
        own[c, Z - TOP] = jnp.zeros((4, 8, 128), F32)
    for c in range(12):
        for z in range(Z - TOP):
            own[c, z, 1:4] = jnp.zeros((3, 8, 128), F32)

    for load in loads[0:3]:
        load.wait()

    @pl.loop(0, Z // 5)
    def _(k):
        for i in range(5):
            z = 5 * k + i
            level = material[z]
            eps_cells = jnp.zeros((8, 128), F32)
            for n in range(8):
                eps_cells = jnp.where(level == n, eps[n], eps_cells)
            fields[COEF, z + 1, 0] = 0.5 / eps_cells

    total = jnp.zeros((8, 128), F32)
    for z in range(Z - TOP):
        tile = fields[COEF, TOP + z + 1, 0]
        own_coef[z, 0] = tile
        total = jnp.where(lane // 8 == z, roll(tile, 8 * z + 4, 1), total)
    edge_coef[...] = total

    pl.semaphore_wait(barrier, len(around) + PLANE - 1 + RING - 1)

    low, high = slice(0, 4), slice(4, 8)
    near = []
    for k, (src, dst, to) in enumerate(
        (
            (own_coef.at[:, 0, high], own_coef.at[:, 2, high], (1, 0)),
            (own_coef.at[:, 0, low], own_coef.at[:, 2, low], (-1, 0)),
            (edge_coef, coef_left.at[0], (0, 1)),
            (edge_coef, coef_right.at[0], (0, -1)),
            (edge_coef.at[high], coef_left.at[1, high], (1, 1)),
            (edge_coef.at[low], coef_left.at[1, low], (-1, 1)),
            (edge_coef.at[high], coef_right.at[1, high], (1, -1)),
            (edge_coef.at[low], coef_right.at[1, low], (-1, -1)),
        )
    ):
        near.append(
            pltpu.make_async_remote_copy(
                src_ref=src, dst_ref=dst, send_sem=coef_send.at[k], recv_sem=coef_recv.at[k],
                device_id=device(*to), device_id_type=MESH,
            )
        )
        near[-1].start()

    for load in loads[3:5]:
        load.wait()

    halos = []
    for part, (lo, hi) in enumerate(GROUPS):
        zs = slice(lo // 2, hi // 2)
        fz = slice(lo + 1, hi + 1)
        plan = [
            (fields.at[:, fz, 0, high], fields.at[:, fz, 2, high], (1, 0)),
            (fields.at[:, fz, 0, low], fields.at[:, fz, 2, low], (-1, 0)),
            (packed.at[0, zs], from_left.at[zs, 0], (0, 1)),
            (packed.at[1, zs], from_right.at[zs, 0], (0, -1)),
            (packed.at[0, zs, high], from_left.at[zs, 1, high], (1, 1)),
            (packed.at[0, zs, low], from_left.at[zs, 1, low], (-1, 1)),
            (packed.at[1, zs, high], from_right.at[zs, 1, high], (1, -1)),
            (packed.at[1, zs, low], from_right.at[zs, 1, low], (-1, -1)),
        ]
        copies = []
        for k, (src, dst, to) in enumerate(plan):
            copies.append(
                pltpu.make_async_remote_copy(
                    src_ref=src, dst_ref=dst, send_sem=halo_send.at[part, k], recv_sem=halo_recv.at[part, k],
                    device_id=device(*to), device_id_type=MESH,
                )
            )
        halos.append(copies)
    for copy in halos[0][:2]:
        copy.start()

    even = lane % 8 < 4

    @pl.loop(0, Z // 4)
    def _(k):
        for i in (0, 1):
            pair = []
            for z in (4 * k + 2 * i, 4 * k + 2 * i + 1):
                total = jnp.zeros((8, 128), F32)
                for c in range(13):
                    total = jnp.where(lane // 8 == c, roll(fields[c, z + 1, 0], 8 * c + 4, 1), total)
                pair.append(total)
            packed[0, 2 * k + i] = jnp.where(even, pair[0], roll(pair[1], 4, 1))
            packed[1, 2 * k + i] = jnp.where(even, roll(pair[0], -4, 1), pair[1])

    for copy in halos[0][2:]:
        copy.start()
    for copy in halos[1]:
        copy.start()

    phase_x = bloch[0]
    phase_y = bloch[1]

    ahead_x = jnp.where(gx == GX - 1, phase_x, 0.0)
    behind_x = jnp.where(gx == 0, -phase_x, 0.0)
    ahead_y = jnp.where(gy == GY - 1, phase_y, 0.0)
    behind_y = jnp.where(gy == 0, -phase_y, 0.0)
    turn_x = jnp.where(sub < 4, ahead_x, behind_x)
    turn_y = jnp.where(lane < 64, ahead_y, behind_y)
    for k, angle in enumerate((turn_y, turn_x, turn_x + turn_y)):
        turn[k, 0] = jnp.cos(angle)
        turn[k, 1] = jnp.sin(angle)

    m = lax.broadcasted_iota(jnp.int32, (SPAN, 128), 0) - SPAN // 2
    lanes = lax.broadcasted_iota(jnp.int32, (SPAN, 128), 1)
    along = lanes % 16
    along = gx * CX + jnp.where(along < 12, along, along - 16)
    angle = 2.0 * math.pi * ((m * along) & (NX - 1)).astype(F32) / NX + phase_x * along.astype(F32) / NX
    wave_x[...] = jnp.where(lanes < 16, jnp.cos(angle), jnp.where(lanes < 32, jnp.sin(angle), 0.0))
    scale = 1.0 / math.sqrt(NX * NY)
    for k, (offset, valid) in enumerate(((lanes, None), (jnp.where(lanes < 64, lanes + CY, lanes - 128), (lanes < 4) | (lanes >= 124)))):
        along = gy * CY + offset
        angle = 2.0 * math.pi * ((m * along) & (NY - 1)).astype(F32) / NY + phase_y * along.astype(F32) / NY
        cos_y = jnp.cos(angle) * scale
        sin_y = jnp.sin(angle) * scale
        if valid is not None:
            cos_y = jnp.where(valid, cos_y, 0.0)
            sin_y = jnp.where(valid, sin_y, 0.0)
        for i in range(3):
            wave_y[i * SPAN : (i + 1) * SPAN, k * 128 : (k + 1) * 128] = cos_y
            wave_y[i * SPAN : (i + 1) * SPAN, 256 + k * 128 : 256 + (k + 1) * 128] = sin_y

    loads[5].wait()
    row16 = lax.broadcasted_iota(jnp.int32, (RING, 128), 0)
    lane16 = lax.broadcasted_iota(jnp.int32, (RING, 128), 1)
    diagonal16 = lane16 // 8 == row16
    by_owner = []
    for which in (0, 1):
        for x_half in range(HALVES):
            rows = [
                orders[which : which + 1, (x_half * RING + r) * 128 : (x_half * RING + r + 1) * 128]
                for r in range(RING)
            ]
            block = jnp.concatenate(rows, 0)
            total = jnp.zeros((RING, 128), jnp.int32)
            for k in range(RING):
                total = total + roll(jnp.where(diagonal16, roll(block, 8 * k, 1), 0), RING - k, 0)
            by_owner.append(total + SPAN // 2)
    for t in range(PLANE):
        x_half, r = divmod(t, RING)
        at = slice(t % WIDE * 128, (t % WIDE + 1) * 128)
        want[0, t // WIDE, :, at] = by_owner[x_half][r : r + 1]
        want[1, t // WIDE, :, at] = by_owner[HALVES + x_half][r : r + 1]

    n = lax.broadcasted_iota(jnp.int32, (SPAN, WIDE * 128), 0)

    @pl.loop(0, PLANE // WIDE)
    def _(t):
        hit = jnp.where(n == want[1, t], 1.0, 0.0).astype(jnp.bfloat16)
        for k in range(3):
            pick_n[t, k * SPAN : (k + 1) * SPAN] = hit

    def unpack(pair):
        for rows in (0, 1):
            left, right = from_left[pair, rows], from_right[pair, rows]
            for i, both in enumerate(
                (jnp.where(even, left, roll(right, 4, 1)), jnp.where(even, roll(left, -4, 1), right))
            ):
                for c in range(13):
                    fields[c, 2 * pair + i + 1, 2 * rows + 1] = roll(both, -(8 * c + 4), 1)
        for z in (2 * pair, 2 * pair + 1):
            turn_halo(z)

    def turn_halo(z):
        for c in (0, 1, 2, 6, 7, 8):
            for k in range(3):
                re = fields[c, z + 1, k + 1]
                im = fields[c + 3, z + 1, k + 1]
                fields[c, z + 1, k + 1] = turn[k, 0] * re - turn[k, 1] * im
                fields[c + 3, z + 1, k + 1] = turn[k, 1] * re + turn[k, 0] * im

    first_sub, last_sub = sub == 0, sub == 7
    first_lane, last_lane = lane == 0, lane == 127

    def shifted(t, shift, axis, seam):
        step = 2 if axis == 0 else 1
        r = [roll(v, shift, axis) for v in t]
        return [jnp.where(seam, r[k ^ step], r[k]) for k in range(4)]

    def updates(held, coef_of):
        def tiles(slot, z):
            return [held[slot, z, k] for k in range(4)]

        def update_h(z):
            for p in (0, 3):
                x, y, w = (tiles(p + c, z) for c in range(3))
                x_up, y_up = (tiles(p + c, z + 1) for c in range(2))
                y_ax = shifted(y, -1, 0, last_sub)
                w_ax = shifted(w, -1, 0, last_sub)
                x_ay = shifted(x, -1, 1, last_lane)
                w_ay = shifted(w, -1, 1, last_lane)
                for k in range(4):
                    cx = w_ay[k] - w[k] - (y_up[k] - y[k])
                    cy = x_up[k] - x[k] - (w_ax[k] - w[k])
                    cz = y_ax[k] - y[k] - (x_ay[k] - x[k])
                    for c, curl in enumerate((cx, cy, cz)):
                        held[6 + p + c, z, k] = held[6 + p + c, z, k] - 0.5 * curl

        def update_e(z):
            coef = [coef_of(z, k) for k in range(4)]
            for p in (0, 3):
                x, y, w = (tiles(6 + p + c, z) for c in range(3))
                x_dn, y_dn = (tiles(6 + p + c, z - 1) for c in range(2))
                y_bx = shifted(y, 1, 0, first_sub)
                w_bx = shifted(w, 1, 0, first_sub)
                x_by = shifted(x, 1, 1, first_lane)
                w_by = shifted(w, 1, 1, first_lane)
                for k in range(4):
                    cx = w[k] - w_by[k] - (y[k] - y_dn[k])
                    cy = x[k] - x_dn[k] - (w[k] - w_bx[k])
                    cz = y[k] - y_bx[k] - (x[k] - x_by[k])
                    for c, curl in enumerate((cx, cy, cz)):
                        held[p + c, z, k] = held[p + c, z, k] + coef[k] * curl

        return update_h, update_e

    update_h, update_e = updates(fields, lambda z, k: fields[COEF, z, k])
    own_h, own_e = updates(own, lambda z, k: own_coef[z, k])

    def over(lo, hi, body, width):
        chunks = (hi - lo) // width

        @pl.loop(0, chunks)
        def _(k):
            for i in range(width):
                body(lo + k * width + i)

        for z in range(lo + chunks * width, hi):
            body(z)

    stores = []

    def advance(group):
        lo, hi = GROUPS[group]
        for copy in halos[group]:
            copy.wait()
        over(lo // 2, hi // 2, unpack, 1)
        for s in range(STEPS):
            above = Z if hi == Z else hi + s
            over((lo + s if lo else 0) + 1, above + 1, update_h, WIDTH)
            above = Z if hi == Z else hi + s + 1
            over((lo + s + 1 if lo else 0) + 1, above + 1, update_e, WIDTH)
        for k, (first, out, rise) in enumerate(((0, e_out, STEPS), (6, h_out, STEPS - 1))):
            zs = slice(lo + rise if lo else 0, Z if hi == Z else hi + rise)
            store = pltpu.make_async_copy(
                fields.at[first : first + 6, zs.start + 1 : zs.stop + 1, 0], out.at[:, zs], store_sem.at[group, k]
            )
            store.start()
            stores.append(store)

    for copy in near:
        copy.wait()
    for rows in (0, 1):
        both = jnp.where(even, coef_left[rows], coef_right[rows])
        for z in range(Z - TOP):
            own_coef[z, 2 * rows + 1] = roll(both, -(8 * z + 4), 1)
    for load in loads[6:8]:
        load.wait()
    for s in range(STEPS):
        for z in range(s, Z - TOP if s < STEPS - 1 else Z - TOP - 1):
            own_h(z)
        for z in range(s + 1, Z - TOP if s < STEPS - 1 else Z - TOP - 1):
            own_e(z)

    flat = []
    at = Z - 2 - TOP
    for c in (0, 1):
        re = [own[c, at, k] for k in range(4)]
        im = [own[c + 3, at, k] for k in range(4)]
        for k in (0, 1):
            flat.append(jnp.concatenate([re[k], re[k + 2], im[k], im[k + 2]], 0))
        for k in (0, 1):
            flat.append(jnp.concatenate([im[k], im[k + 2], -re[k], -re[k + 2]], 0))
    plane = jnp.concatenate(flat, 1)
    sums = jnp.dot(wave_x[:, 0:32], plane, precision=lax.Precision.HIGHEST, preferred_element_type=F32)
    re0, im0, re1, im1 = (sums[:, k * 256 : (k + 1) * 256] for k in range(4))
    left = jnp.concatenate(
        [
            jnp.concatenate([re0, re1, im0, im1], 0),
            jnp.concatenate([im0, im1, -re0, -re1], 0),
        ],
        1,
    )
    table = lax.dot_general(
        left, wave_y[...], (((1,), (1,)), ((), ())), precision=lax.Precision.HIGHEST, preferred_element_type=F32
    )
    high = table.astype(jnp.bfloat16).astype(F32)
    rest = table - high
    middle = rest.astype(jnp.bfloat16).astype(F32)
    low = rest - middle
    column = lax.broadcasted_iota(jnp.int32, table.shape, 1)
    split_a[...] = jnp.where(column < SPAN, high, jnp.where(column < 2 * SPAN, middle, low)).astype(jnp.bfloat16)

    @pl.loop(0, PLANE // WIDE)
    def _(d):
        t = (place // WIDE + d) % (PLANE // WIDE)
        by_m = jnp.dot(split_a[...], pick_n[t], preferred_element_type=F32)
        hit = n == want[0, t]
        found = [
            jnp.sum(jnp.where(hit, by_m[r * SPAN : (r + 1) * SPAN], 0.0), 0, keepdims=True) for r in (0, 2, 1, 3)
        ]
        found = jnp.concatenate(found, 0)
        for k in range(WIDE):
            parts[t * WIDE + k] = found[:, k * 128 : (k + 1) * 128]
        for k in range(WIDE):
            to = t * WIDE + k

            @pl.when(to != place)
            def _():
                pltpu.make_async_remote_copy(
                    src_ref=parts.at[to], dst_ref=got_parts.at[place], send_sem=part_send, recv_sem=part_recv,
                    device_id=plane_device(to), device_id_type=MESH,
                ).start()

    for copy in halos[2]:
        copy.start()
    advance(0)
    advance(1)
    got_parts[place] = parts[place]
    pltpu.make_async_copy(got_parts.at[0 : PLANE - 1], got_parts.at[0 : PLANE - 1], part_recv).wait()
    mine = jnp.sum(got_parts[...], 0)

    tall = jnp.concatenate([mine, jnp.zeros((RING - 4, 128), F32)], 0)
    rows = jnp.zeros((RING, 128), F32)
    for k in range(RING):
        rows = rows + roll(jnp.where(diagonal16, roll(tall, 8 * k, 1), 0.0), RING - k, 0)
    for r in range(RING):
        pieces[r] = rows[r : r + 1]

    @pl.loop(1, RING)
    def _(d):
        to = (ring + d) % RING
        pltpu.make_async_remote_copy(
            src_ref=pieces.at[to], dst_ref=got_pieces.at[ring], send_sem=piece_send, recv_sem=piece_recv,
            device_id=ring_device(to), device_id_type=MESH,
        ).start()

    got_pieces[ring] = pieces[ring]

    advance(2)
    pltpu.make_async_copy(got_pieces.at[0 : RING - 1], got_pieces.at[0 : RING - 1], piece_recv).wait()
    total = jnp.broadcast_to(jnp.sum(got_pieces[...], 0), (8, 128))
    rows = total
    for r in range(1, 4):
        rows = jnp.where(sub == r, roll(total, -8 * r, 1), rows)
    amp_out[...] = rows

    pltpu.make_async_copy(parts.at[0 : PLANE - 1], parts.at[0 : PLANE - 1], part_send).wait()
    pltpu.make_async_copy(pieces.at[0 : RING - 1], pieces.at[0 : RING - 1], piece_send).wait()
    for store in stores:
        store.wait()


def hand_over(e_in, h_in, amp_in, e_out, h_out, amp_out, held, in_sems, out_sems):
    ends = [(e_in, e_out, c) for c in range(6)] + [(h_in, h_out, c) for c in range(6)]
    loads = [pltpu.make_async_copy(src.at[c], held.at[k], in_sems.at[k]) for k, (src, _, c) in enumerate(ends)]
    stores = [pltpu.make_async_copy(held.at[k], dst.at[c], out_sems.at[k]) for k, (_, dst, c) in enumerate(ends)]
    for load in loads:
        load.start()
    amp_out[...] = amp_in[0:4, 0:8]
    for load, store in zip(loads, stores):
        load.wait()
        store.start()
    for store in stores:
        store.wait()


def per_device(e_field, h_field, material, eps_table, bloch_phase, orders):
    vmem = pl.BlockSpec(memory_space=pltpu.VMEM)
    hbm = pl.BlockSpec(memory_space=pltpu.HBM)
    e_next, h_next, amplitudes = pl.pallas_call(
        kernel,
        out_shape=(
            jax.ShapeDtypeStruct(e_field.shape, F32),
            jax.ShapeDtypeStruct(h_field.shape, F32),
            jax.ShapeDtypeStruct((8, 128), F32),
        ),
        in_specs=[hbm] * 6,
        out_specs=(hbm, hbm, vmem),
        scratch_shapes=[
            pltpu.VMEM((13, Z + 2, 4, 8, 128), F32),
            pltpu.VMEM((Z, 8, 128), jnp.int32),
            pltpu.VMEM((2, 4096), jnp.int32),
            pltpu.SMEM((8,), F32),
            pltpu.SMEM((2,), F32),
            pltpu.VMEM((2, Z // 2, 8, 128), F32),
            pltpu.VMEM((Z // 2, 2, 8, 128), F32),
            pltpu.VMEM((Z // 2, 2, 8, 128), F32),
            pltpu.VMEM((3, 2, 8, 128), F32),
            pltpu.VMEM((12, Z - TOP + 1, 4, 8, 128), F32),
            pltpu.VMEM((Z - TOP, 4, 8, 128), F32),
            pltpu.VMEM((8, 128), F32),
            pltpu.VMEM((2, 8, 128), F32),
            pltpu.VMEM((2, 8, 128), F32),
            pltpu.VMEM((SPAN, 128), F32),
            pltpu.VMEM((3 * SPAN, 512), F32),
            pltpu.VMEM((PLANE // WIDE, 3 * SPAN, WIDE * 128), jnp.bfloat16),
            pltpu.VMEM((2, PLANE // WIDE, 1, WIDE * 128), jnp.int32),
            pltpu.VMEM((4 * SPAN, 3 * SPAN), jnp.bfloat16),
            pltpu.VMEM((PLANE, 4, 128), F32),
            pltpu.VMEM((PLANE, 4, 128), F32),
            pltpu.VMEM((RING, 1, 128), F32),
            pltpu.VMEM((RING, 1, 128), F32),
            pltpu.SemaphoreType.DMA((8,)),
            pltpu.SemaphoreType.DMA((len(GROUPS), 2)),
            pltpu.SemaphoreType.DMA((8,)),
            pltpu.SemaphoreType.DMA((8,)),
            pltpu.SemaphoreType.DMA((len(GROUPS), 8)),
            pltpu.SemaphoreType.DMA((len(GROUPS), 8)),
            pltpu.SemaphoreType.DMA,
            pltpu.SemaphoreType.DMA,
            pltpu.SemaphoreType.DMA,
            pltpu.SemaphoreType.DMA,
        ],
        compiler_params=pltpu.CompilerParams(
            collective_id=0, has_side_effects=True, vmem_limit_bytes=60 * 2**20
        ),
    )(e_field, h_field, material, eps_table, bloch_phase, orders)
    return pl.pallas_call(
        hand_over,
        out_shape=(
            jax.ShapeDtypeStruct(e_field.shape, F32),
            jax.ShapeDtypeStruct(h_field.shape, F32),
            jax.ShapeDtypeStruct((4, 8), F32),
        ),
        in_specs=[hbm, hbm, vmem],
        out_specs=(hbm, hbm, vmem),
        scratch_shapes=[
            pltpu.VMEM((12,) + e_field.shape[1:], F32),
            pltpu.SemaphoreType.DMA((12,)),
            pltpu.SemaphoreType.DMA((12,)),
        ],
        compiler_params=pltpu.CompilerParams(vmem_limit_bytes=60 * 2**20),
    )(e_next, h_next, amplitudes)


def solution(mesh):
    return jax.shard_map(
        per_device,
        mesh=mesh,
        in_specs=(
            P(None, None, "gx", "gy"),
            P(None, None, "gx", "gy"),
            P(None, "gx", "gy"),
            P(),
            P(),
            P(),
        ),
        out_specs=(P(None, None, "gx", "gy"), P(None, None, "gx", "gy"), P(None, ("gx", "gy"))),
        check_vma=False,
    )
```
